256 devices in a mesh: dp: 2 (over core), ctx: 16 (over z, x_lo), tp: 8 (over y, x_hi).
Axes of the slice: x: 4 (x_hi: 2, x_lo: 2; x = x_hi * 2 + x_lo), y: 4, z: 8, core: 2. Of those that a mesh axis runs over, the one named last changes fastest.
Arguments:
- queries: bfloat16 [2, 8192, 4096], P('dp', 'ctx', 'tp'), may hold values from -6 to 6
- keys: bfloat16 [2, 8192, 1024], P('dp', 'ctx', 'tp'), may hold values from -6 to 6
- values: bfloat16 [2, 8192, 1024], P('dp', 'ctx', 'tp'), may hold values from -6 to 6
- document_lengths: int32 [2, 16], P('dp'), may hold values from 1 to 4096, 8192 in all within a row
- out_weight: bfloat16 [4096, 5120], P('tp', 'dp'), may hold values from -0.09375 to 0.09375
Outputs:
- projected: bfloat16 [2, 8192, 5120], P('dp', 'ctx', 'tp')
The draws below stay inside these ranges and needn't reach their ends.
Inputs may be any that keep to these rules, and one draw needn't show every extreme that they name: `document_lengths`: each row sums to 8192; its largest entry is exactly 4096.
All inputs are finite; a program needn't handle non-finite values.
Results may differ from the reference program's by a relative error of at most 0.015.
Values may be sent and summed in bfloat16 or wider, within the bound.
A program may use at most 64 MiB of HBM per device.

```python
import math
import jax
import jax.numpy as jnp
import numpy as np
from jax import lax

D = 5120
QUERY_HEADS = 32
KEY_VALUE_HEADS = 8
HEAD_SIZE = 128
NDOCS = 16
ROW_POSITIONS = 8192
PACKED_ROWS = 2
MAXDOC = 4096
N_TP = 8


def draw_queries(key, part):
    key = jax.random.fold_in(key, 1)
    return jnp.clip(jax.random.normal(key, (PACKED_ROWS, ROW_POSITIONS, QUERY_HEADS * HEAD_SIZE), jnp.float32), -5.0, 5.0).astype(jnp.bfloat16)


def draw_keys(key, part):
    key = jax.random.fold_in(key, 2)
    return jnp.clip(jax.random.normal(key, (PACKED_ROWS, ROW_POSITIONS, KEY_VALUE_HEADS * HEAD_SIZE), jnp.float32), -5.0, 5.0).astype(jnp.bfloat16)


def block_levels(key, shape, cuts, smallest, top_value):
    factor_of = 1.0
    for axis_at, blocks in cuts:
        draws = jax.random.uniform(jax.random.fold_in(jax.random.fold_in(key, 6), axis_at), (blocks,), jnp.float32, smallest / len(cuts), top_value / len(cuts))
        factor_of = factor_of * jnp.repeat(jnp.exp(draws), shape[axis_at] // blocks).reshape((-1,) + (1,) * (len(shape) - 1 - axis_at))
    return factor_of


def length_profile(number_of, total, reach, lean):
    weights = [(1 << 20) // math.isqrt(rank ** lean) + 1 for rank in range(2, number_of + 1)]
    spare, given = total - reach - (number_of - 1), [1] * (number_of - 1)
    while spare > 0:
        movable = [i for i in range(number_of - 1) if given[i] < reach]
        mass, left = sum([weights[i] for i in movable]), spare
        for i in movable:
            extra = min(reach - given[i], max(1, left * weights[i] // mass), spare)
            given[i] = given[i] + extra
            spare = spare - extra
    return np.array([reach] + given)


def ragged_sizes(rng, number_of, total, bound, lean):
    if number_of == 2:
        one = jax.random.randint(rng, (), max(1, total - bound), min(bound, total - 1) + 1)
        return jnp.stack([one, total - one])
    lengths = jnp.asarray(length_profile(number_of, total, bound, lean), jnp.int32)
    twos = (number_of - 1) // 2
    giver, receiver = lengths[1:1 + 2 * twos:2], lengths[2:2 + 2 * twos:2]
    margin = jnp.minimum(giver - 1, bound - receiver)
    passed = jax.random.randint(jax.random.fold_in(rng, 1), (twos,), 0, 1 << 20) % (margin + 1)
    lengths = lengths.at[1:1 + 2 * twos:2].set(giver - passed).at[2:2 + 2 * twos:2].set(receiver + passed)
    return lengths[jax.random.permutation(jax.random.fold_in(rng, 2), number_of)]


def scatter_about(rng, shape, width, limit, cuts=(), held_as=jnp.bfloat16):
    values = jax.random.normal(rng, shape, jnp.float32) * width
    if len(cuts) > 0:
        values = block_levels(rng, shape, cuts, -0.22, 0.18) * values
    return jnp.clip(values, min=-limit, max=limit).astype(held_as)


def setup_inputs(seed: int = 0) -> dict:
    arg_keys = jax.random.split(jax.random.key(seed), 6)
    queries = draw_queries(jax.random.fold_in(arg_keys[5], 71), 0)
    keys = draw_keys(jax.random.fold_in(arg_keys[5], 71), 0)
    values = scatter_about(arg_keys[2], (PACKED_ROWS, ROW_POSITIONS, KEY_VALUE_HEADS * HEAD_SIZE), 1.0, 6.0, ((0, 2), (1, 16), (2, 8)))
    document_lengths = jax.vmap(lambda own: ragged_sizes(own, NDOCS, ROW_POSITIONS, MAXDOC, 2))(jax.random.split(arg_keys[3], PACKED_ROWS)).reshape((PACKED_ROWS, NDOCS)).astype(jnp.int32)
    out_weight = scatter_about(arg_keys[4], (QUERY_HEADS * HEAD_SIZE, D), (QUERY_HEADS * HEAD_SIZE) ** -0.5, 0.09375, ((0, 8), (1, 2)))
    return {"queries": queries, "keys": keys, "values": values, "document_lengths": document_lengths, "out_weight": out_weight}


def document_of(positions, doc_ends):
    return jnp.sum((positions[:, None] >= doc_ends[None, :]).astype(jnp.int32), axis=1)


def attend_row(query_row_slice, key_row_slice, value_row_slice, length_row):
    doc_ends = jnp.cumsum(length_row).astype(jnp.int32)
    heads_per_group = QUERY_HEADS // KEY_VALUE_HEADS
    block_rows = math.gcd(ROW_POSITIONS, 256)
    window = min(ROW_POSITIONS, MAXDOC + block_rows)
    query_tensor = query_row_slice.reshape(ROW_POSITIONS, KEY_VALUE_HEADS, heads_per_group, HEAD_SIZE)
    key_tensor = key_row_slice.reshape(ROW_POSITIONS, KEY_VALUE_HEADS, HEAD_SIZE)
    value_tensor = value_row_slice.reshape(ROW_POSITIONS, KEY_VALUE_HEADS, HEAD_SIZE)

    def one_block(block_index):
        query_first = (block_index * block_rows).astype(jnp.int32)
        key_first = jnp.clip(query_first + block_rows - window, 0, ROW_POSITIONS - window).astype(jnp.int32)
        query_part = lax.dynamic_slice_in_dim(query_tensor, query_first, block_rows, 0).astype(jnp.float32)
        key_part = lax.dynamic_slice_in_dim(key_tensor, key_first, window, 0).astype(jnp.float32)
        value_part = lax.dynamic_slice_in_dim(value_tensor, key_first, window, 0).astype(jnp.float32)
        query_pos = query_first + jnp.arange(block_rows, dtype=jnp.int32)
        key_pos = key_first + jnp.arange(window, dtype=jnp.int32)
        allowed = (key_pos[None, :] <= query_pos[:, None]) & (
            document_of(key_pos, doc_ends)[None, :] == document_of(query_pos, doc_ends)[:, None])
        scores = jnp.einsum("qhgd,khd->hgqk", query_part, key_part) * (HEAD_SIZE ** -0.5)
        peak = jnp.max(jnp.where(allowed, scores, -1e30), axis=-1)
        weights = jnp.where(allowed, jnp.exp(scores - peak[..., None]), 0.0)
        denom = jnp.sum(weights, axis=-1)
        rounded = lax.optimization_barrier(weights.astype(jnp.bfloat16)).astype(jnp.float32)
        blended_output = jnp.einsum("hgqk,khd->hgqd", rounded, value_part) / denom[..., None]
        blended_output = jnp.transpose(blended_output, (2, 0, 1, 3))
        return blended_output.reshape(block_rows, QUERY_HEADS * HEAD_SIZE).astype(jnp.bfloat16)

    blocks = lax.map(one_block, jnp.arange(ROW_POSITIONS // block_rows, dtype=jnp.int32))
    return blocks.reshape(ROW_POSITIONS, QUERY_HEADS * HEAD_SIZE)


def reference(queries, keys, values, document_lengths, out_weight):
    outputs = []
    share = QUERY_HEADS * HEAD_SIZE // N_TP
    for row_index in range(PACKED_ROWS):
        attended = attend_row(queries[row_index], keys[row_index], values[row_index], document_lengths[row_index])
        summed = jnp.zeros((ROW_POSITIONS, D), jnp.float32)
        for group_index in range(N_TP):
            partial_term = jnp.dot(attended[:, group_index * share:(group_index + 1) * share],
                                   out_weight[group_index * share:(group_index + 1) * share],
                                   preferred_element_type=jnp.float32)
            summed = summed + partial_term.astype(jnp.bfloat16).astype(jnp.float32)
        outputs.append(summed.astype(jnp.bfloat16))
    return jnp.stack(outputs)
```

```python
import functools

import jax
import jax.numpy as jnp
from jax import lax
from jax.experimental import pallas as pl
from jax.experimental.pallas import tpu as pltpu
from jax.sharding import PartitionSpec as P

HEAD = 128
LOG2E = 1.4426950408889634
APART = 16384.0
MESH = pl.DeviceIdType.MESH


def kernel(
    shape, q_hbm, k_hbm, v_hbm, lens, w_hbm, out_hbm,
    qv, kc, vc, qd, qc, sc, mx, acc, att, wb, mine, give, take, outv,
    loc_sem, zs, zr, xs, xr, ws, wr, fs, fr, ags, agr, fws, fwr, rss, rsr, outs,
):
    ncore, nctx, ntp, rows, heads, chunk = shape
    nchunk = rows // chunk
    half = chunk // 2
    stacked = heads * chunk
    cols = wb.shape[2] // 2
    slots = kc.shape[0]
    hops = (slots - 1) // 2
    ny = ntp // 2

    core, ctx, tp = lax.axis_index("dp"), lax.axis_index("ctx"), lax.axis_index("tp")
    lo = ctx % 2
    y, hi = tp // 2, tp % 2
    up = (core, (ctx + 2) % nctx, tp)
    down = (core, (ctx + nctx - 2) % nctx, tp)
    pair = (core, ctx + 1 - 2 * lo, tp)
    yp = (core, ctx, (tp + 2) % ntp)
    ym = (core, ctx, (tp + ntp - 2) % ntp)
    yo = (core, ctx, (tp + 4) % ntp)
    mate = (core, ctx, tp + 1 - 2 * hi)
    twin = (1 - core, ctx, tp)

    barrier = pltpu.get_barrier_semaphore()
    peers = (up, down, pair, yp, ym, yo, mate, twin)
    for peer in peers:
        pl.semaphore_signal(barrier, inc=1, device_id=peer, device_id_type=MESH)
    pl.semaphore_wait(barrier, len(peers))

    def remote(src, dst, send, recv, dev):
        return pltpu.make_async_remote_copy(
            src_ref=src, dst_ref=dst, send_sem=send, recv_sem=recv, device_id=dev, device_id_type=MESH
        )

    bank = (kc, vc)
    inputs = (k_hbm, v_hbm)

    def z_copy(j, p, src=None):
        src = bank[p].at[2 * j - 2, :, 0:HEAD] if src is None else src
        return remote(src, bank[p].at[2 * j, :, 0:HEAD], zs.at[j - 1, p], zr.at[j - 1, p], up)

    def x_copy(i, p, src=None):
        src = bank[p].at[2 * i + 2 * lo, :, 0:HEAD] if src is None else src
        return remote(src, bank[p].at[2 * i + 1, :, 0:HEAD], xs.at[i, p], xr.at[i, p], pair)

    for p in range(2):
        z_copy(1, p, inputs[p].at[0]).start()

        @pl.when(lo == 0)
        def _():
            x_copy(0, p, inputs[p].at[0]).start()

    own = [pltpu.make_async_copy(inputs[p].at[0], bank[p].at[0, :, 0:HEAD], loc_sem.at[p]) for p in range(2)]
    own.append(pltpu.make_async_copy(q_hbm.at[0], qv, loc_sem.at[2]))
    for c in own:
        c.start()

    has_cols = (y // 2) == core

    def w_copy(i, dst_tp):
        return remote(w_hbm.at[:, pl.ds(i * 2 * cols, 2 * cols)], wb.at[y], ws.at[i], wr.at[y], (core, ctx, dst_tp))

    def w_here(i):
        return pltpu.make_async_copy(w_hbm.at[:, pl.ds(i * 2 * cols, 2 * cols)], wb.at[y], loc_sem.at[3])

    for i in range(2):
        dst_y = 2 * core + i

        @pl.when(dst_y != y)
        def _():
            w_copy(i, dst_y * 2 + hi).start()

        @pl.when(dst_y == y)
        def _():
            w_here(i).start()

    lane = lax.broadcasted_iota(jnp.int32, (1, HEAD), 1)
    ends = jnp.zeros((1, HEAD), jnp.int32)
    starts = jnp.zeros((1, HEAD), jnp.int32)
    for j in range(lens.shape[1]):
        ends = ends + jnp.where(lane >= j, lens[0, j], 0)
        starts = starts + jnp.where(lane > j, lens[0, j], 0)
    ends = jnp.where(lane < lens.shape[1], ends, 0)

    def in_doc(first):
        pos = first + lax.broadcasted_iota(jnp.int32, (rows, HEAD), 0)
        return (pos >= starts) & (pos < ends)

    qd[...] = jnp.where(in_doc(ctx * rows), APART, 0.0).astype(jnp.bfloat16)

    def mark(d, carry):
        kc[d, :, HEAD:] = jnp.where(in_doc((ctx - d) * rows), 0.0, -1.0).astype(jnp.bfloat16)
        vc[d, :, HEAD:] = jnp.ones((rows, HEAD), jnp.bfloat16)
        return carry

    lax.fori_loop(0, slots, mark, 0)

    for j in range(1, hops + 1):
        for p in range(2):
            z_copy(j, p).wait_recv()
            if j < hops:
                z_copy(j + 1, p).start()
                x_copy(j - lo, p).start()
            else:

                @pl.when(lo == 1)
                def _():
                    x_copy(hops - 1, p).start()

    for c in own:
        c.wait()
    for i in range(hops):
        for p in range(2):
            x_copy(i, p).wait_recv()

    scale = LOG2E * HEAD ** (-0.5)
    dims = (((1,), (1,)), ((), ()))

    def scores(d):
        return lax.dot_general(qc[...], kc[d], dims, preferred_element_type=jnp.float32)

    def lane_max(s):
        m = s[:, 0:HEAD]
        for g in range(1, rows // HEAD):
            m = jnp.maximum(m, s[:, g * HEAD : (g + 1) * HEAD])
        return m

    def attend(c):
        first = pl.multiple_of(c * chunk, chunk)
        for h in range(heads):
            qc[h * chunk : (h + 1) * chunk, 0:HEAD] = qv[pl.ds(first, chunk), h * HEAD : (h + 1) * HEAD]
            qc[h * chunk : (h + 1) * chunk, HEAD:] = qd[pl.ds(first, chunk), :]
        s = scores(0)
        row = lax.broadcasted_iota(jnp.int32, (stacked, rows), 0) % chunk + first
        col = lax.broadcasted_iota(jnp.int32, (stacked, rows), 1)
        s = jnp.where(col <= row, s, -1e30)
        sc[0] = s
        mx[...] = lane_max(s)

        def score_step(d, carry):
            t = scores(d)
            sc[d] = t
            mx[...] = jnp.maximum(mx[...], lane_max(t))
            return carry

        lax.fori_loop(1, slots, score_step, 0)
        peak = jnp.max(mx[...], axis=1, keepdims=True) * scale
        mx[...] = jnp.broadcast_to(peak, mx.shape)
        acc[...] = jnp.zeros_like(acc)

        def value_step(d, carry):
            top = mx[:, 0:1]
            w16 = jnp.exp2(sc[d] * scale - top).astype(jnp.bfloat16)
            acc[...] += jnp.dot(w16, vc[d], preferred_element_type=jnp.float32)
            return carry

        lax.fori_loop(0, slots, value_step, 0)
        for h in range(heads):
            part = acc[h * chunk : (h + 1) * chunk, 0:HEAD] / acc[h * chunk : (h + 1) * chunk, HEAD:]
            att[y, pl.ds(first, chunk), h * HEAD : (h + 1) * HEAD] = part.astype(jnp.bfloat16)

    def at_y(k):
        return lax.rem(y + k, ny)

    def spread(c, way):
        rng = pl.ds(pl.multiple_of(c * chunk, chunk), chunk)
        ref = att.at[y, rng]
        return remote(ref, ref, ags.at[way, c], agr.at[way, c], (yp, ym)[way])

    def spread_in(c, way):
        rng = pl.ds(pl.multiple_of(c * chunk, chunk), chunk)
        ref = att.at[at_y(ny - 1 if way == 0 else 1), rng]
        return remote(ref, ref, ags.at[way, c], agr.at[way, c], (yp, ym)[way])

    def pass_on(c, way):
        rng = pl.ds(pl.multiple_of(c * chunk + way * half, half), half)
        ref = att.at[at_y(ny - 1 if way == 0 else 1), rng]
        return remote(ref, ref, fws.at[way, c], fwr.at[way, c], (yp, ym)[way])

    def pass_in(c, way):
        rng = pl.ds(pl.multiple_of(c * chunk + way * half, half), half)
        ref = att.at[at_y(2), rng]
        return remote(ref, ref, fws.at[way, c], fwr.at[way, c], (yp, ym)[way])

    def swap(c):
        rng = pl.ds(pl.multiple_of(c * chunk, chunk), chunk)
        return remote(give.at[rng], take.at[rng], rss.at[c], rsr.at[c], mate)

    def to_out(c):
        rng = pl.ds(pl.multiple_of(c * chunk, chunk), chunk)
        return pltpu.make_async_copy(outv.at[rng], out_hbm.at[0, rng], outs.at[c])

    def w_share(g):
        return remote(wb.at[g], wb.at[g], fs.at[g], fr.at[g], twin)

    def product(c, side):
        rng = pl.ds(pl.multiple_of(c * chunk, chunk), chunk)
        first = pl.multiple_of(side * cols, HEAD)
        total = jnp.dot(att[0, rng, :], wb[0, :, pl.ds(first, cols)], preferred_element_type=jnp.float32)
        for g in range(1, ny):
            total += jnp.dot(att[g, rng, :], wb[g, :, pl.ds(first, cols)], preferred_element_type=jnp.float32)
        return total

    def step(it, carry):
        @pl.when(it < nchunk)
        def _():
            attend(it)
            for way in range(2):
                spread(it, way).start()

        @pl.when((it == 0) & has_cols)
        def _():
            for i in range(2):

                @pl.when(2 * core + i == y)
                def _():
                    w_here(i).wait()

            w_share(y).start()
            for k in range(1, ny):
                g = at_y(k)
                remote(wb.at[g], wb.at[g], ws.at[0], wr.at[g], yp).wait_recv()
                w_share(g).start()

        @pl.when((it >= 1) & (it <= nchunk))
        def _():
            for way in range(2):
                spread_in(it - 1, way).wait_recv()
                pass_on(it - 1, way).start()

        @pl.when((it == 2) & jnp.logical_not(has_cols))
        def _():
            for g in range(ny):
                w_share(g).wait_recv()

        @pl.when((it >= 2) & (it <= nchunk + 1))
        def _():
            c = it - 2
            rng = pl.ds(pl.multiple_of(c * chunk, chunk), chunk)
            for way in range(2):
                pass_in(c, way).wait_recv()
            give[rng, :] = product(c, 1 - hi).astype(jnp.bfloat16)
            swap(c).start()
            mine[rng, :] = product(c, hi)

        @pl.when(it >= 3)
        def _():
            c = it - 3
            rng = pl.ds(pl.multiple_of(c * chunk, chunk), chunk)
            swap(c).wait_recv()
            outv[rng, :] = (mine[rng, :] + take[rng, :].astype(jnp.float32)).astype(jnp.bfloat16)
            to_out(c).start()

        return carry

    lax.fori_loop(0, nchunk + 3, step, 0)

    for j in range(1, hops + 1):
        for p in range(2):
            z_copy(j, p).wait_send()
            x_copy(j - 1, p).wait_send()
    for i in range(2):

        @pl.when(2 * core + i != y)
        def _():
            w_copy(i, tp).wait_send()

    @pl.when(has_cols)
    def _():
        for g in range(ny):
            w_share(g).wait_send()

    def drain(c, carry):
        for way in range(2):
            spread(c, way).wait_send()
            pass_on(c, way).wait_send()
        swap(c).wait_send()
        to_out(c).wait()
        return carry

    lax.fori_loop(0, nchunk, drain, 0)


def shards(ncore, nctx, ntp, queries, keys, values, document_lengths, out_weight):
    rows = queries.shape[1]
    heads = queries.shape[2] // keys.shape[2]
    depth = out_weight.shape[0]
    cols = out_weight.shape[1] * ncore // ntp
    chunk = 128
    nchunk = rows // chunk
    hops = 4
    slots = 2 * hops + 1
    ny = ntp // 2
    bf16, f32 = jnp.bfloat16, jnp.float32
    dma = pltpu.SemaphoreType.DMA
    any_spec = pl.BlockSpec(memory_space=pl.ANY)
    return pl.pallas_call(
        functools.partial(kernel, (ncore, nctx, ntp, rows, heads, chunk)),
        out_shape=jax.ShapeDtypeStruct((1, rows, cols), bf16),
        in_specs=[any_spec, any_spec, any_spec, pl.BlockSpec(memory_space=pltpu.SMEM), any_spec],
        out_specs=any_spec,
        scratch_shapes=[
            pltpu.VMEM((rows, heads * HEAD), bf16),
            pltpu.VMEM((slots, rows, 2 * HEAD), bf16),
            pltpu.VMEM((slots, rows, 2 * HEAD), bf16),
            pltpu.VMEM((rows, HEAD), bf16),
            pltpu.VMEM((heads * chunk, 2 * HEAD), bf16),
            pltpu.VMEM((slots, heads * chunk, rows), f32),
            pltpu.VMEM((heads * chunk, HEAD), f32),
            pltpu.VMEM((heads * chunk, 2 * HEAD), f32),
            pltpu.VMEM((ny, rows, heads * HEAD), bf16),
            pltpu.VMEM((ny, depth, 2 * cols), bf16),
            pltpu.VMEM((rows, cols), f32),
            pltpu.VMEM((rows, cols), bf16),
            pltpu.VMEM((rows, cols), bf16),
            pltpu.VMEM((rows, cols), bf16),
            dma((4,)),
            dma((hops, 2)), dma((hops, 2)), dma((hops, 2)), dma((hops, 2)),
            dma((2,)), dma((ny,)), dma((ny,)), dma((ny,)),
            dma((2, nchunk)), dma((2, nchunk)), dma((2, nchunk)), dma((2, nchunk)),
            dma((nchunk,)), dma((nchunk,)), dma((nchunk,)),
        ],
        compiler_params=pltpu.CompilerParams(
            collective_id=0, has_side_effects=True, vmem_limit_bytes=56 * 1024 * 1024
        ),
        name="attend_project",
    )(queries, keys, values, document_lengths, out_weight)


def solution(mesh):
    sizes = (mesh.shape["dp"], mesh.shape["ctx"], mesh.shape["tp"])
    in_specs = (P("dp", "ctx", "tp"), P("dp", "ctx", "tp"), P("dp", "ctx", "tp"), P("dp", None), P("tp", "dp"))
    return jax.shard_map(
        functools.partial(shards, *sizes), mesh=mesh, in_specs=in_specs, out_specs=P("dp", "ctx", "tp"), check_vma=False
    )
```

```python
import functools

import jax
import jax.numpy as jnp
from jax import lax
from jax.experimental import pallas as pl
from jax.experimental.pallas import tpu as pltpu
from jax.sharding import PartitionSpec as P

HEAD = 128
LOG2E = 1.4426950408889634
APART = 16384.0
MESH = pl.DeviceIdType.MESH


def kernel(
    shape, q_hbm, k_hbm, v_hbm, lens, w_hbm, mine_hbm, take_hbm,
    qv, kc, vc, kd, qd, qc, sc, mx, acc, att, wb, mine, give,
    loc_sem, zs, zr, xs, xr, ws, wr, fs, fr, ags, agr, fws, fwr, rss, rsr, outs,
):
    ncore, nctx, ntp, rows, heads, chunk = shape
    nchunk = rows // chunk
    half = chunk // 2
    stacked = heads * chunk
    cols = wb.shape[2] // 2
    slots = kc.shape[0]
    hops = (slots - 1) // 2
    ny = ntp // 2
    parts = zs.shape[1] // 2
    span = rows // parts
    wparts = fs.shape[1]
    wspan = rows // wparts

    core, ctx, tp = lax.axis_index("dp"), lax.axis_index("ctx"), lax.axis_index("tp")
    z, lo = ctx // 2, ctx % 2
    nz = nctx // 2
    y, hi = tp // 2, tp % 2
    up = (core, (ctx + 2) % nctx, tp)
    down = (core, (ctx + nctx - 2) % nctx, tp)
    pair = (core, ctx + 1 - 2 * lo, tp)
    yp = (core, ctx, (tp + 2) % ntp)
    ym = (core, ctx, (tp + ntp - 2) % ntp)
    yo = (core, ctx, (tp + 4) % ntp)
    mate = (core, ctx, tp + 1 - 2 * hi)
    twin = (1 - core, ctx, tp)

    barrier = pltpu.get_barrier_semaphore()
    peers = (pair, yp, ym, yo, mate, twin)

    def greet(peer):
        pl.semaphore_signal(barrier, inc=1, device_id=peer, device_id_type=MESH)

    for peer in peers:
        greet(peer)

    @pl.when(z < nz - 1)
    def _():
        greet(up)

    @pl.when(z > 0)
    def _():
        greet(down)


    def remote(src, dst, send, recv, dev):
        return pltpu.make_async_remote_copy(
            src_ref=src, dst_ref=dst, send_sem=send, recv_sem=recv, device_id=dev, device_id_type=MESH
        )

    def at_y(k):
        return lax.rem(y + k, ny)

    bank = (kc, vc)
    inputs = (k_hbm, v_hbm)

    def piece(ref, p):
        return ref.at[pl.ds((p % parts) * span, span)]

    def z_copy(j, p):
        which = bank[p // parts]
        src = inputs[p // parts].at[0] if j == 1 else which.at[2 * j - 2]
        return remote(piece(src, p), piece(which.at[2 * j], p), zs.at[j - 1, p], zr.at[j - 1, p], up)

    def x_copy(i, p, own=False):
        which = bank[p // parts]
        src = inputs[p // parts].at[0] if own else which.at[2 * i + 2 * lo]
        return remote(piece(src, p), piece(which.at[2 * i + 1], p), xs.at[i, p], xr.at[i, p], pair)

    own = [pltpu.make_async_copy(inputs[p].at[0], bank[p].at[0], loc_sem.at[p]) for p in range(2)]
    own.append(pltpu.make_async_copy(q_hbm.at[0], qv, loc_sem.at[2]))
    for c in own:
        c.start()

    has_cols = (y // 2) == core

    def w_rows(ref, r):
        return ref.at[pl.ds(r * wspan, wspan)]

    def w_copy(i, r, dst_tp):
        src = w_hbm.at[pl.ds(r * wspan, wspan), pl.ds(i * 2 * cols, 2 * cols)]
        return remote(src, w_rows(wb.at[y], r), ws.at[i, r], wr.at[y, r], (core, ctx, dst_tp))

    def w_in(g, r):
        return remote(w_rows(wb.at[g], r), w_rows(wb.at[g], r), ws.at[0, r], wr.at[g, r], yp)

    def w_here(i):
        return pltpu.make_async_copy(w_hbm.at[:, pl.ds(i * 2 * cols, 2 * cols)], wb.at[y], loc_sem.at[3])

    def w_share(g, r):
        return remote(w_rows(wb.at[g], r), w_rows(wb.at[g], r), fs.at[g, r], fr.at[g, r], twin)

    for i in range(2):

        @pl.when(2 * core + i == y)
        def _():
            w_here(i).start()

    lane = lax.broadcasted_iota(jnp.int32, (1, HEAD), 1)
    ends = jnp.zeros((1, HEAD), jnp.int32)
    starts = jnp.zeros((1, HEAD), jnp.int32)
    for j in range(lens.shape[1]):
        ends = ends + jnp.where(lane >= j, lens[0, j], 0)
        starts = starts + jnp.where(lane > j, lens[0, j], 0)
    ends = jnp.where(lane < lens.shape[1], ends, 0)

    def in_doc(first):
        pos = first + lax.broadcasted_iota(jnp.int32, (rows, HEAD), 0)
        return (pos >= starts) & (pos < ends)

    qd[...] = jnp.where(in_doc(ctx * rows), APART, 0.0).astype(jnp.bfloat16)

    def mark(d, carry):
        kd[d] = jnp.where(in_doc((ctx - d) * rows), 0.0, -1.0).astype(jnp.bfloat16)

        @pl.when(d > ctx)
        def _():
            kc[d] = jnp.zeros((rows, HEAD), jnp.bfloat16)
            vc[d] = jnp.zeros((rows, HEAD), jnp.bfloat16)

        return carry

    lax.fori_loop(0, slots, mark, 0)

    scale = LOG2E * HEAD ** (-0.5)
    dims = (((1,), (1,)), ((), ()))

    def load_queries(c):
        first = pl.multiple_of(c * chunk, chunk)
        for h in range(heads):
            qc[h * chunk : (h + 1) * chunk, 0:HEAD] = qv[pl.ds(first, chunk), h * HEAD : (h + 1) * HEAD]
            qc[h * chunk : (h + 1) * chunk, HEAD:] = qd[pl.ds(first, chunk), :]

    def score_tile(d, first):
        s = lax.dot_general(qc[...], jnp.concatenate([kc[d], kd[d]], axis=1), dims, preferred_element_type=jnp.float32)
        if d == 0:
            row = lax.broadcasted_iota(jnp.int32, (stacked, rows), 0) % chunk + first
            col = lax.broadcasted_iota(jnp.int32, (stacked, rows), 1)
            s = jnp.where(col <= row, s, -1e30)
        sc[:, d * rows : (d + 1) * rows] = s
        m = s[:, 0:HEAD]
        for g in range(1, rows // HEAD):
            m = jnp.maximum(m, s[:, g * HEAD : (g + 1) * HEAD])
        mx[...] = jnp.maximum(mx[...], m)

    ones = jnp.ones((rows, HEAD), jnp.bfloat16)

    def value_tile(d, peak):
        w16 = jnp.exp2(sc[:, d * rows : (d + 1) * rows] * scale - peak).astype(jnp.bfloat16)
        acc[...] += jnp.dot(w16, jnp.concatenate([vc[d], ones], axis=1), preferred_element_type=jnp.float32)

    for c in own:
        c.wait()
    load_queries(0)
    mx[...] = jnp.full(mx.shape, -1e30, jnp.float32)

    pl.semaphore_wait(barrier, len(peers) + jnp.where(z > 0, 1, 0) + jnp.where(z < nz - 1, 1, 0))

    def z_sends(j):
        return (z >= j - 1) & (z < nz - 1)

    def x_sends(i):
        return z >= i + lo

    def x_comes(i):
        return z >= i + 1 - lo

    for p in range(2 * parts):

        @pl.when(z_sends(1))
        def _():
            z_copy(1, p).start()

        @pl.when(lo == 0)
        def _():
            x_copy(0, p, True).start()

    for r in range(wparts):
        for i in range(2):
            dst_y = 2 * core + i

            @pl.when(dst_y != y)
            def _():
                w_copy(i, r, dst_y * 2 + hi).start()

    score_tile(0, 0)

    def weights_on(r):
        @pl.when(has_cols)
        def _():
            for k in range(1, ny):
                g = at_y(k)
                w_in(g, r).wait_recv()
                w_share(g, r).start()

    @pl.when(has_cols)
    def _():
        for i in range(2):

            @pl.when(2 * core + i == y)
            def _():
                w_here(i).wait()

        for r in range(wparts):
            w_share(y, r).start()

    for j in range(1, hops + 1):
        for p in range(2 * parts):

            @pl.when(z >= j)
            def _():
                z_copy(j, p).wait_recv()

            if j < hops:

                @pl.when(z_sends(j + 1))
                def _():
                    z_copy(j + 1, p).start()

                @pl.when(x_sends(j - lo))
                def _():
                    x_copy(j - lo, p).start()
            else:

                @pl.when((lo == 1) & x_sends(hops - 1))
                def _():
                    x_copy(hops - 1, p).start()

        score_tile(2 * j, 0)
        if j >= 2:
            for p in range(2 * parts):

                @pl.when(x_comes(j - 2))
                def _():
                    x_copy(j - 2, p).wait_recv()

            score_tile(2 * j - 3, 0)
            if j - 2 < wparts - 1:
                weights_on(j - 2)
    for p in range(2 * parts):

        @pl.when(x_comes(hops - 1))
        def _():
            x_copy(hops - 1, p).wait_recv()

    score_tile(2 * hops - 1, 0)

    def attend(c):
        acc[...] = jnp.zeros_like(acc)
        peak = jnp.max(mx[...], axis=1, keepdims=True) * scale

        @pl.when(c < nchunk - 1)
        def _():
            load_queries(c + 1)
            mx[...] = jnp.full(mx.shape, -1e30, jnp.float32)
            for d in range(slots):
                value_tile(d, peak)
                score_tile(d, (c + 1) * chunk)

        @pl.when(c == nchunk - 1)
        def _():
            for d in range(slots):
                value_tile(d, peak)

        first = pl.multiple_of(c * chunk, chunk)
        for h in range(heads):
            part = acc[h * chunk : (h + 1) * chunk, 0:HEAD] / acc[h * chunk : (h + 1) * chunk, HEAD:]
            att[y, pl.ds(first, chunk), h * HEAD : (h + 1) * HEAD] = part.astype(jnp.bfloat16)

    def spread(c, way):
        rng = pl.ds(pl.multiple_of(c * chunk, chunk), chunk)
        ref = att.at[y, rng]
        return remote(ref, ref, ags.at[way, c], agr.at[way, c], (yp, ym)[way])

    def spread_in(c, way):
        rng = pl.ds(pl.multiple_of(c * chunk, chunk), chunk)
        ref = att.at[at_y(ny - 1 if way == 0 else 1), rng]
        return remote(ref, ref, ags.at[way, c], agr.at[way, c], (yp, ym)[way])

    def pass_on(c, way):
        rng = pl.ds(pl.multiple_of(c * chunk + way * half, half), half)
        ref = att.at[at_y(ny - 1 if way == 0 else 1), rng]
        return remote(ref, ref, fws.at[way, c], fwr.at[way, c], (yp, ym)[way])

    def pass_in(c, way):
        rng = pl.ds(pl.multiple_of(c * chunk + way * half, half), half)
        ref = att.at[at_y(2), rng]
        return remote(ref, ref, fws.at[way, c], fwr.at[way, c], (yp, ym)[way])

    def swap(c):
        rng = pl.ds(pl.multiple_of(c * chunk, chunk), chunk)
        return remote(give.at[rng], take_hbm.at[rng], rss.at[c], rsr.at[c], mate)

    def to_out(c):
        rng = pl.ds(pl.multiple_of(c * chunk, chunk), chunk)
        return pltpu.make_async_copy(mine.at[rng], mine_hbm.at[rng], outs.at[c])

    def product(c, side):
        rng = pl.ds(pl.multiple_of(c * chunk, chunk), chunk)
        first = pl.multiple_of(side * cols, HEAD)
        total = jnp.dot(att[0, rng, :], wb[0, :, pl.ds(first, cols)], preferred_element_type=jnp.float32)
        for g in range(1, ny):
            total += jnp.dot(att[g, rng, :], wb[g, :, pl.ds(first, cols)], preferred_element_type=jnp.float32)
        return total

    def step(it, carry):
        @pl.when(it < nchunk)
        def _():
            attend(it)
            for way in range(2):
                spread(it, way).start()

        @pl.when(it == 0)
        def _():
            weights_on(wparts - 1)

        @pl.when((it >= 1) & (it <= nchunk))
        def _():
            for way in range(2):
                spread_in(it - 1, way).wait_recv()
                pass_on(it - 1, way).start()

        @pl.when((it == 2) & jnp.logical_not(has_cols))
        def _():
            for g in range(ny):
                for r in range(wparts):
                    w_share(g, r).wait_recv()

        @pl.when((it >= 2) & (it <= nchunk + 1))
        def _():
            c = it - 2
            rng = pl.ds(pl.multiple_of(c * chunk, chunk), chunk)
            for way in range(2):
                pass_in(c, way).wait_recv()
            give[rng, :] = product(c, 1 - hi).astype(jnp.bfloat16)
            swap(c).start()
            mine[rng, :] = product(c, hi)
            to_out(c).start()

        return carry

    lax.fori_loop(0, nchunk + 2, step, 0)

    for j in range(1, hops + 1):
        for p in range(2 * parts):

            @pl.when(z_sends(j))
            def _():
                z_copy(j, p).wait_send()

            @pl.when(x_sends(j - 1))
            def _():
                x_copy(j - 1, p).wait_send()
    for r in range(wparts):
        for i in range(2):

            @pl.when(2 * core + i != y)
            def _():
                w_copy(i, r, tp).wait_send()

    @pl.when(has_cols)
    def _():
        for g in range(ny):
            for r in range(wparts):
                w_share(g, r).wait_send()

    def drain(c, carry):
        for way in range(2):
            spread(c, way).wait_send()
            pass_on(c, way).wait_send()
        swap(c).wait()
        to_out(c).wait()
        return carry

    lax.fori_loop(0, nchunk, drain, 0)


def shards(ncore, nctx, ntp, queries, keys, values, document_lengths, out_weight):
    rows = queries.shape[1]
    heads = queries.shape[2] // keys.shape[2]
    depth = out_weight.shape[0]
    cols = out_weight.shape[1] * ncore // ntp
    chunk = 128
    nchunk = rows // chunk
    hops = 4
    slots = 2 * hops + 1
    parts, wparts = 2, 4
    ny = ntp // 2
    bf16, f32 = jnp.bfloat16, jnp.float32
    dma = pltpu.SemaphoreType.DMA
    any_spec = pl.BlockSpec(memory_space=pl.ANY)
    mine, take = pl.pallas_call(
        functools.partial(kernel, (ncore, nctx, ntp, rows, heads, chunk)),
        out_shape=(jax.ShapeDtypeStruct((rows, cols), f32), jax.ShapeDtypeStruct((rows, cols), bf16)),
        in_specs=[any_spec, any_spec, any_spec, pl.BlockSpec(memory_space=pltpu.SMEM), any_spec],
        out_specs=(any_spec, any_spec),
        scratch_shapes=[
            pltpu.VMEM((rows, heads * HEAD), bf16),
            pltpu.VMEM((slots, rows, HEAD), bf16),
            pltpu.VMEM((slots, rows, HEAD), bf16),
            pltpu.VMEM((slots, rows, HEAD), bf16),
            pltpu.VMEM((rows, HEAD), bf16),
            pltpu.VMEM((heads * chunk, 2 * HEAD), bf16),
            pltpu.VMEM((heads * chunk, slots * rows), f32),
            pltpu.VMEM((heads * chunk, HEAD), f32),
            pltpu.VMEM((heads * chunk, 2 * HEAD), f32),
            pltpu.VMEM((ny, rows, heads * HEAD), bf16),
            pltpu.VMEM((ny, depth, 2 * cols), bf16),
            pltpu.VMEM((rows, cols), f32),
            pltpu.VMEM((rows, cols), bf16),
            dma((4,)),
            dma((hops, 2 * parts)), dma((hops, 2 * parts)), dma((hops, 2 * parts)), dma((hops, 2 * parts)),
            dma((2, wparts)), dma((ny, wparts)), dma((ny, wparts)), dma((ny, wparts)),
            dma((2, nchunk)), dma((2, nchunk)), dma((2, nchunk)), dma((2, nchunk)),
            dma((nchunk,)), dma((nchunk,)), dma((nchunk,)),
        ],
        compiler_params=pltpu.CompilerParams(
            collective_id=0, has_side_effects=True, vmem_limit_bytes=56 * 1024 * 1024
        ),
        name="attend_project",
    )(queries, keys, values, document_lengths, out_weight)
    return (mine + take.astype(f32)).astype(bf16)[None]


def solution(mesh):
    sizes = (mesh.shape["dp"], mesh.shape["ctx"], mesh.shape["tp"])
    in_specs = (P("dp", "ctx", "tp"), P("dp", "ctx", "tp"), P("dp", "ctx", "tp"), P("dp", None), P("tp", "dp"))
    return jax.shard_map(
        functools.partial(shards, *sizes), mesh=mesh, in_specs=in_specs, out_specs=P("dp", "ctx", "tp"), check_vma=False
    )
```

```python
import functools

import jax
import jax.numpy as jnp
from jax import lax
from jax.experimental import pallas as pl
from jax.experimental.pallas import tpu as pltpu
from jax.sharding import PartitionSpec as P

HEAD = 128
LOG2E = 1.4426950408889634
APART = 16384.0
MESH = pl.DeviceIdType.MESH


def kernel(
    shape, q_hbm, k_hbm, v_hbm, lens, w_hbm, mine_hbm, take_hbm,
    qv, kc, vc, kd, qd, qc, sc, mx, acc, att, wb, mine, give,
    loc_sem, zs, zr, xs, xr, ws, wr, fs, fr, ags, agr, fws, fwr, rss, rsr, outs,
):
    ncore, nctx, ntp, rows, heads, chunk = shape
    nchunk = rows // chunk
    half = chunk // 2
    stacked = heads * chunk
    cols = wb.shape[2] // 2
    slots = kc.shape[0]
    hops = (slots - 1) // 2
    ny = ntp // 2
    parts = zs.shape[1] // 2
    span = rows // parts
    wparts = fs.shape[1]
    wspan = rows // wparts

    core, ctx, tp = lax.axis_index("dp"), lax.axis_index("ctx"), lax.axis_index("tp")
    z, lo = ctx // 2, ctx % 2
    nz = nctx // 2
    y, hi = tp // 2, tp % 2
    up = (core, (ctx + 2) % nctx, tp)
    down = (core, (ctx + nctx - 2) % nctx, tp)
    pair = (core, ctx + 1 - 2 * lo, tp)
    yp = (core, ctx, (tp + 2) % ntp)
    ym = (core, ctx, (tp + ntp - 2) % ntp)
    yo = (core, ctx, (tp + 4) % ntp)
    mate = (core, ctx, tp + 1 - 2 * hi)
    twin = (1 - core, ctx, tp)

    barrier = pltpu.get_barrier_semaphore()
    peers = (pair, yp, ym, yo, mate, twin)

    def greet(peer):
        pl.semaphore_signal(barrier, inc=1, device_id=peer, device_id_type=MESH)

    for peer in peers:
        greet(peer)

    @pl.when(z < nz - 1)
    def _():
        greet(up)

    @pl.when(z > 0)
    def _():
        greet(down)


    def remote(src, dst, send, recv, dev):
        return pltpu.make_async_remote_copy(
            src_ref=src, dst_ref=dst, send_sem=send, recv_sem=recv, device_id=dev, device_id_type=MESH
        )

    def at_y(k):
        return lax.rem(y + k, ny)

    bank = (kc, vc)
    inputs = (k_hbm, v_hbm)

    def piece(ref, p):
        return ref.at[pl.ds((p % parts) * span, span)]

    def z_copy(j, p):
        which = bank[p // parts]
        src = inputs[p // parts].at[0] if j == 1 else which.at[2 * j - 2]
        return remote(piece(src, p), piece(which.at[2 * j], p), zs.at[j - 1, p], zr.at[j - 1, p], up)

    def x_copy(i, p, own=False):
        which = bank[p // parts]
        src = inputs[p // parts].at[0] if own else which.at[2 * i + 2 * lo]
        return remote(piece(src, p), piece(which.at[2 * i + 1], p), xs.at[i, p], xr.at[i, p], pair)

    own = [pltpu.make_async_copy(inputs[p].at[0], bank[p].at[0], loc_sem.at[p]) for p in range(2)]
    own.append(pltpu.make_async_copy(q_hbm.at[0], qv, loc_sem.at[2]))
    for c in own:
        c.start()

    has_cols = (y // 2) == core

    def w_rows(ref, r):
        return ref.at[pl.ds(r * wspan, wspan)]

    def w_copy(i, r, dst_tp):
        src = w_hbm.at[pl.ds(r * wspan, wspan), pl.ds(i * 2 * cols, 2 * cols)]
        return remote(src, w_rows(wb.at[y], r), ws.at[i, r], wr.at[y, r], (core, ctx, dst_tp))

    def w_in(g, r):
        return remote(w_rows(wb.at[g], r), w_rows(wb.at[g], r), ws.at[0, r], wr.at[g, r], yp)

    def w_here(i):
        return pltpu.make_async_copy(w_hbm.at[:, pl.ds(i * 2 * cols, 2 * cols)], wb.at[y], loc_sem.at[3])

    def w_share(g, r):
        return remote(w_rows(wb.at[g], r), w_rows(wb.at[g], r), fs.at[g, r], fr.at[g, r], twin)

    for i in range(2):

        @pl.when(2 * core + i == y)
        def _():
            w_here(i).start()

    lane = lax.broadcasted_iota(jnp.int32, (1, HEAD), 1)
    ends = jnp.zeros((1, HEAD), jnp.int32)
    starts = jnp.zeros((1, HEAD), jnp.int32)
    for j in range(lens.shape[1]):
        ends = ends + jnp.where(lane >= j, lens[0, j], 0)
        starts = starts + jnp.where(lane > j, lens[0, j], 0)
    ends = jnp.where(lane < lens.shape[1], ends, 0)

    def in_doc(first):
        pos = first + lax.broadcasted_iota(jnp.int32, (rows, HEAD), 0)
        return (pos >= starts) & (pos < ends)

    qd[...] = jnp.where(in_doc(ctx * rows), APART, 0.0).astype(jnp.bfloat16)

    def mark(d, carry):
        kd[d] = jnp.where(in_doc((ctx - d) * rows), 0.0, -1.0).astype(jnp.bfloat16)

        @pl.when(d > ctx)
        def _():
            kc[d] = jnp.zeros((rows, HEAD), jnp.bfloat16)
            vc[d] = jnp.zeros((rows, HEAD), jnp.bfloat16)

        return carry

    lax.fori_loop(0, slots, mark, 0)

    scale = LOG2E * HEAD ** (-0.5)
    dims = (((1,), (1,)), ((), ()))

    def load_queries(c):
        first = pl.multiple_of(c * chunk, chunk)
        for h in range(heads):
            qc[h * chunk : (h + 1) * chunk, 0:HEAD] = qv[pl.ds(first, chunk), h * HEAD : (h + 1) * HEAD]
            qc[h * chunk : (h + 1) * chunk, HEAD:] = qd[pl.ds(first, chunk), :]

    def score_tile(d, first):
        s = lax.dot_general(qc[...], jnp.concatenate([kc[d], kd[d]], axis=1), dims, preferred_element_type=jnp.float32)
        if d == 0:
            row = lax.broadcasted_iota(jnp.int32, (stacked, rows), 0) % chunk + first
            col = lax.broadcasted_iota(jnp.int32, (stacked, rows), 1)
            s = jnp.where(col <= row, s, -1e30)
        sc[:, d * rows : (d + 1) * rows] = s
        m = s[:, 0:HEAD]
        for g in range(1, rows // HEAD):
            m = jnp.maximum(m, s[:, g * HEAD : (g + 1) * HEAD])
        mx[...] = jnp.maximum(mx[...], m)

    ones = jnp.ones((rows, HEAD), jnp.bfloat16)

    def value_tile(d, peak):
        w16 = jnp.exp2(sc[:, d * rows : (d + 1) * rows] * scale - peak).astype(jnp.bfloat16)
        acc[...] += jnp.dot(w16, jnp.concatenate([vc[d], ones], axis=1), preferred_element_type=jnp.float32)

    for c in own:
        c.wait()
    load_queries(0)
    mx[...] = jnp.full(mx.shape, -1e30, jnp.float32)

    pl.semaphore_wait(barrier, len(peers) + jnp.where(z > 0, 1, 0) + jnp.where(z < nz - 1, 1, 0))

    def z_sends(j):
        return (z >= j - 1) & (z < nz - 1)

    def x_sends(i):
        return z >= i + lo

    def x_comes(i):
        return z >= i + 1 - lo

    for p in range(2 * parts):

        @pl.when(z_sends(1))
        def _():
            z_copy(1, p).start()

        @pl.when(lo == 0)
        def _():
            x_copy(0, p, True).start()

    for r in range(wparts):
        for i in range(2):
            dst_y = 2 * core + i

            @pl.when(dst_y != y)
            def _():
                w_copy(i, r, dst_y * 2 + hi).start()

    score_tile(0, 0)

    def weights_on(r):
        @pl.when(has_cols)
        def _():
            for k in range(1, ny):
                g = at_y(k)
                w_in(g, r).wait_recv()
                w_share(g, r).start()

    @pl.when(has_cols)
    def _():
        for i in range(2):

            @pl.when(2 * core + i == y)
            def _():
                w_here(i).wait()

        for r in range(wparts):
            w_share(y, r).start()

    for j in range(1, hops + 1):
        for p in range(2 * parts):

            @pl.when(z >= j)
            def _():
                z_copy(j, p).wait_recv()

            if j < hops:

                @pl.when(z_sends(j + 1))
                def _():
                    z_copy(j + 1, p).start()

                @pl.when(x_sends(j - lo))
                def _():
                    x_copy(j - lo, p).start()
            else:

                @pl.when((lo == 1) & x_sends(hops - 1))
                def _():
                    x_copy(hops - 1, p).start()

        score_tile(2 * j, 0)
        if j >= 2:
            for p in range(2 * parts):

                @pl.when(x_comes(j - 2))
                def _():
                    x_copy(j - 2, p).wait_recv()

            score_tile(2 * j - 3, 0)
            if j - 2 < wparts - 1:
                weights_on(j - 2)
    for p in range(2 * parts):

        @pl.when(x_comes(hops - 1))
        def _():
            x_copy(hops - 1, p).wait_recv()

    score_tile(2 * hops - 1, 0)

    def attend(c):
        acc[...] = jnp.zeros_like(acc)
        peak = jnp.max(mx[...], axis=1, keepdims=True) * scale

        @pl.when(c < nchunk - 1)
        def _():
            load_queries(c + 1)
            mx[...] = jnp.full(mx.shape, -1e30, jnp.float32)
            for d in range(slots):
                value_tile(d, peak)
                score_tile(d, (c + 1) * chunk)

        @pl.when(c == nchunk - 1)
        def _():
            for d in range(slots):
                value_tile(d, peak)

        first = pl.multiple_of(c * chunk, chunk)
        for h in range(heads):
            part = acc[h * chunk : (h + 1) * chunk, 0:HEAD] / acc[h * chunk : (h + 1) * chunk, HEAD:]
            att[y, pl.ds(first, chunk), h * HEAD : (h + 1) * HEAD] = part.astype(jnp.bfloat16)

    def spread(c, way):
        rng = pl.ds(pl.multiple_of(c * chunk, chunk), chunk)
        ref = att.at[y, rng]
        return remote(ref, ref, ags.at[way, c], agr.at[way, c], (yp, ym)[way])

    def spread_in(c, way):
        rng = pl.ds(pl.multiple_of(c * chunk, chunk), chunk)
        ref = att.at[at_y(ny - 1 if way == 0 else 1), rng]
        return remote(ref, ref, ags.at[way, c], agr.at[way, c], (yp, ym)[way])

    def pass_on(c, way):
        rng = pl.ds(pl.multiple_of(c * chunk + way * half, half), half)
        ref = att.at[at_y(ny - 1 if way == 0 else 1), rng]
        return remote(ref, ref, fws.at[way, c], fwr.at[way, c], (yp, ym)[way])

    def pass_in(c, way):
        rng = pl.ds(pl.multiple_of(c * chunk + way * half, half), half)
        ref = att.at[at_y(2), rng]
        return remote(ref, ref, fws.at[way, c], fwr.at[way, c], (yp, ym)[way])

    last = nchunk - 1

    def across(g):
        ref = att.at[g, pl.ds(last * chunk, chunk)]
        return remote(ref, ref, fws.at[0, last], fwr.at[0, last], yo)

    def swap(c):
        rng = pl.ds(pl.multiple_of(c * chunk, chunk), chunk)
        return remote(give.at[rng], take_hbm.at[rng], rss.at[c], rsr.at[c], mate)

    def to_out(c):
        rng = pl.ds(pl.multiple_of(c * chunk, chunk), chunk)
        return pltpu.make_async_copy(mine.at[rng], mine_hbm.at[rng], outs.at[c])

    def product(c, side):
        rng = pl.ds(pl.multiple_of(c * chunk, chunk), chunk)
        first = pl.multiple_of(side * cols, HEAD)
        total = jnp.dot(att[0, rng, :], wb[0, :, pl.ds(first, cols)], preferred_element_type=jnp.float32)
        for g in range(1, ny):
            total += jnp.dot(att[g, rng, :], wb[g, :, pl.ds(first, cols)], preferred_element_type=jnp.float32)
        return total

    def step(it, carry):
        @pl.when(it < nchunk)
        def _():
            attend(it)
            for way in range(2):
                spread(it, way).start()

            @pl.when(it == last)
            def _():
                across(y).start()

        @pl.when(it == 0)
        def _():
            weights_on(wparts - 1)

        @pl.when((it >= 1) & (it <= nchunk))
        def _():
            for way in range(2):
                spread_in(it - 1, way).wait_recv()

                @pl.when(it - 1 < last)
                def _():
                    pass_on(it - 1, way).start()

        @pl.when((it == 2) & jnp.logical_not(has_cols))
        def _():
            for g in range(ny):
                for r in range(wparts):
                    w_share(g, r).wait_recv()

        @pl.when((it >= 2) & (it <= nchunk + 1))
        def _():
            c = it - 2
            rng = pl.ds(pl.multiple_of(c * chunk, chunk), chunk)

            @pl.when(c < last)
            def _():
                for way in range(2):
                    pass_in(c, way).wait_recv()

            @pl.when(c == last)
            def _():
                across(at_y(2)).wait_recv()

            give[rng, :] = product(c, 1 - hi).astype(jnp.bfloat16)
            swap(c).start()
            mine[rng, :] = product(c, hi).astype(jnp.bfloat16)
            to_out(c).start()

        return carry

    lax.fori_loop(0, nchunk + 2, step, 0)

    for j in range(1, hops + 1):
        for p in range(2 * parts):

            @pl.when(z_sends(j))
            def _():
                z_copy(j, p).wait_send()

            @pl.when(x_sends(j - 1))
            def _():
                x_copy(j - 1, p).wait_send()
    for r in range(wparts):
        for i in range(2):

            @pl.when(2 * core + i != y)
            def _():
                w_copy(i, r, tp).wait_send()

    @pl.when(has_cols)
    def _():
        for g in range(ny):
            for r in range(wparts):
                w_share(g, r).wait_send()

    def drain(c, carry):
        for way in range(2):
            spread(c, way).wait_send()

            @pl.when(c < last)
            def _():
                pass_on(c, way).wait_send()

        swap(c).wait()
        to_out(c).wait()
        return carry

    lax.fori_loop(0, nchunk, drain, 0)
    across(y).wait_send()


def shards(ncore, nctx, ntp, queries, keys, values, document_lengths, out_weight):
    rows = queries.shape[1]
    heads = queries.shape[2] // keys.shape[2]
    depth = out_weight.shape[0]
    cols = out_weight.shape[1] * ncore // ntp
    chunk = 128
    nchunk = rows // chunk
    hops = 4
    slots = 2 * hops + 1
    parts, wparts = 2, 4
    ny = ntp // 2
    bf16, f32 = jnp.bfloat16, jnp.float32
    dma = pltpu.SemaphoreType.DMA
    any_spec = pl.BlockSpec(memory_space=pl.ANY)
    mine, take = pl.pallas_call(
        functools.partial(kernel, (ncore, nctx, ntp, rows, heads, chunk)),
        out_shape=(jax.ShapeDtypeStruct((rows, cols), bf16), jax.ShapeDtypeStruct((rows, cols), bf16)),
        in_specs=[any_spec, any_spec, any_spec, pl.BlockSpec(memory_space=pltpu.SMEM), any_spec],
        out_specs=(any_spec, any_spec),
        scratch_shapes=[
            pltpu.VMEM((rows, heads * HEAD), bf16),
            pltpu.VMEM((slots, rows, HEAD), bf16),
            pltpu.VMEM((slots, rows, HEAD), bf16),
            pltpu.VMEM((slots, rows, HEAD), bf16),
            pltpu.VMEM((rows, HEAD), bf16),
            pltpu.VMEM((heads * chunk, 2 * HEAD), bf16),
            pltpu.VMEM((heads * chunk, slots * rows), f32),
            pltpu.VMEM((heads * chunk, HEAD), f32),
            pltpu.VMEM((heads * chunk, 2 * HEAD), f32),
            pltpu.VMEM((ny, rows, heads * HEAD), bf16),
            pltpu.VMEM((ny, depth, 2 * cols), bf16),
            pltpu.VMEM((rows, cols), bf16),
            pltpu.VMEM((rows, cols), bf16),
            dma((4,)),
            dma((hops, 2 * parts)), dma((hops, 2 * parts)), dma((hops, 2 * parts)), dma((hops, 2 * parts)),
            dma((2, wparts)), dma((ny, wparts)), dma((ny, wparts)), dma((ny, wparts)),
            dma((2, nchunk)), dma((2, nchunk)), dma((2, nchunk)), dma((2, nchunk)),
            dma((nchunk,)), dma((nchunk,)), dma((nchunk,)),
        ],
        compiler_params=pltpu.CompilerParams(
            collective_id=0, has_side_effects=True, vmem_limit_bytes=56 * 1024 * 1024
        ),
        name="attend_project",
    )(queries, keys, values, document_lengths, out_weight)
    return (mine.astype(f32) + take.astype(f32)).astype(bf16)[None]


def solution(mesh):
    sizes = (mesh.shape["dp"], mesh.shape["ctx"], mesh.shape["tp"])
    in_specs = (P("dp", "ctx", "tp"), P("dp", "ctx", "tp"), P("dp", "ctx", "tp"), P("dp", None), P("tp", "dp"))
    return jax.shard_map(
        functools.partial(shards, *sizes), mesh=mesh, in_specs=in_specs, out_specs=P("dp", "ctx", "tp"), check_vma=False
    )
```
